256 devices in a mesh: freq: 4 (over x), row: 8 (over y, core), col: 8 (over z).
Axes of the slice: x: 4, y: 4, z: 8, core: 2. Of those that a mesh axis runs over, the one named last changes fastest.
Arguments:
- operator: bfloat16 [4, 2, 12000, 12000], P('freq', None, 'row', 'col'), may hold values from -0.0390625 to 0.0390625
- recorded: bfloat16 [4, 2, 12000, 128], P('freq', None, 'row'), may hold values from -61 to 61
Outputs:
- solution: float32 [4, 2, 12000, 128], P('freq', None, 'col')
- residual: float32 [4, 2, 12000, 128], P('freq', None, 'row')
The draws below stay inside these ranges and needn't reach their ends.
All inputs are finite; a program needn't handle non-finite values.
Results may differ from the reference program's by a relative error of at most 0.0044.
Values sent between devices are 32-bit elements; how exact they have to be, the bound alone decides.
A program may use at most 128 MiB of HBM per device.

```python
import math
import jax
import jax.numpy as jnp

NF = 4
NR = 12000
NS = 128
ITERS = 2


def draw_recorded(key, part):
    key = jax.random.fold_in(key, 7)
    key_base, key_rough, key_source = jax.random.split(key, 3)
    base = jnp.clip(jax.random.normal(key_base, (NF, 2, NR, NS), jnp.float32), -4.0, 4.0)
    rough = jnp.exp(jax.random.uniform(key_rough, (NF, 1, NR, 1), jnp.float32, 0.0, math.log(2.0)))
    source = jnp.exp(jax.random.uniform(key_source, (1, 1, 1, NS), jnp.float32, 0.0, math.log(10.0))) / 3.0
    freq_rise = 0.5 + jnp.arange(NF, dtype=jnp.float32).reshape(NF, 1, 1, 1) / max(NF - 1, 1)
    recv_rise = 0.5 + jnp.arange(NR, dtype=jnp.float32).reshape(1, 1, NR, 1) / NR
    return (base * rough * source * freq_rise * recv_rise).astype(jnp.bfloat16)


def block_levels(stream_key, shape, cuts, least, high):
    factor_of = 1.0
    for dim, blocks in cuts:
        heights = jax.random.uniform(jax.random.fold_in(jax.random.fold_in(stream_key, 6), dim), (blocks,), jnp.float32, least / len(cuts), high / len(cuts))
        factor_of = factor_of * jnp.repeat(jnp.exp(heights), shape[dim] // blocks).reshape((-1,) + (1,) * (len(shape) - 1 - dim))
    return factor_of


def noise(key, extent, deviation, bound, cuts=(), kind=jnp.bfloat16):
    result = jax.random.normal(key, extent, jnp.float32) * deviation
    if len(cuts) > 0:
        result = block_levels(key, extent, cuts, -0.22, 0.18) * result
    return jnp.clip(result, min=-bound, max=bound).astype(kind)


def setup_inputs(seed: int = 0) -> dict:
    streams_of = jax.random.split(jax.random.key(seed), 3)
    return {
        "operator": noise(streams_of[0], (NF, 2, NR, NR), (2 * NR) ** -0.5, 0.0390625, ((0, 4), (2, 8), (3, 8))),
        "recorded": draw_recorded(jax.random.fold_in(streams_of[2], 71), 0),
    }


epsilon = 1e-06

def forward_apply(operator, vector):
    pieces = []
    for freq_index in range(NF):
        real_op = operator[freq_index, 0]
        imag_op = operator[freq_index, 1]
        real_vec = vector[freq_index, 0]
        imag_vec = vector[freq_index, 1]
        real_out = jnp.dot(real_op, real_vec, preferred_element_type=jnp.float32) - jnp.dot(imag_op, imag_vec, preferred_element_type=jnp.float32)
        imag_out = jnp.dot(real_op, imag_vec, preferred_element_type=jnp.float32) + jnp.dot(imag_op, real_vec, preferred_element_type=jnp.float32)
        pieces.append(jnp.stack([real_out, imag_out]))
    return jnp.stack(pieces)

def adjoint_apply(operator, vector):
    pieces = []
    for freq_index in range(NF):
        real_op = operator[freq_index, 0].T
        imag_op = operator[freq_index, 1].T
        real_vec = vector[freq_index, 0]
        imag_vec = vector[freq_index, 1]
        real_out = jnp.dot(real_op, real_vec, preferred_element_type=jnp.float32) + jnp.dot(imag_op, imag_vec, preferred_element_type=jnp.float32)
        imag_out = jnp.dot(real_op, imag_vec, preferred_element_type=jnp.float32) - jnp.dot(imag_op, real_vec, preferred_element_type=jnp.float32)
        pieces.append(jnp.stack([real_out, imag_out]))
    return jnp.stack(pieces)

def field_norm(field):
    return jnp.sqrt(jnp.sum(field * field) + epsilon)

def reference(operator, recorded):
    observed = recorded.astype(jnp.float32)
    beta_now = field_norm(observed)
    left_vec = observed / beta_now
    back = adjoint_apply(operator, left_vec.astype(jnp.bfloat16))
    alpha_now = field_norm(back)
    right_vec = back / alpha_now
    search = right_vec
    phi_bar = beta_now
    rho_bar = alpha_now
    solution = jnp.zeros((NF, 2, NR, NS), jnp.float32)
    fitted = jnp.zeros((NF, 2, NR, NS), jnp.float32)
    search_image = fitted
    w_ratio = jnp.float32(0.0)
    for turn_index in range(ITERS):
        imaged = forward_apply(operator, right_vec.astype(jnp.bfloat16))
        update = imaged - alpha_now * left_vec
        beta_now = field_norm(update)
        left_vec = update / beta_now
        if turn_index == 0:
            search_image = imaged
        else:
            search_image = imaged - w_ratio * search_image
        rho_now = jnp.sqrt(rho_bar * rho_bar + beta_now * beta_now)
        cosine = rho_bar / rho_now
        sine_val = beta_now / rho_now
        phi_now = cosine * phi_bar
        phi_bar = sine_val * phi_bar
        solution = solution + phi_now / rho_now * search
        fitted = fitted + phi_now / rho_now * search_image
        if turn_index + 1 < ITERS:
            back = adjoint_apply(operator, left_vec.astype(jnp.bfloat16)) - beta_now * right_vec
            alpha_now = field_norm(back)
            right_vec = back / alpha_now
            w_ratio = sine_val * alpha_now / rho_now
            rho_bar = -cosine * alpha_now
            search = right_vec - w_ratio * search
    return (solution, observed - fitted)
```

```python
import jax
import jax.numpy as jnp
from jax import lax
from jax.experimental import pallas as pl
from jax.experimental.pallas import tpu as pltpu
from jax.sharding import PartitionSpec as P

MESH = pl.DeviceIdType.MESH
EPS = 1e-06
N = 1500
NP = 1536
LAST = N - 11 * 128
ZC = NP // 8
F32, BF16 = jnp.float32, jnp.bfloat16
MESSAGES = 192


def dot(a, b):
    return lax.dot_general(a, b, (((1,), (0,)), ((), ())), preferred_element_type=F32)


def turn(x):
    lane = lax.broadcasted_iota(jnp.int32, x.shape, 1)
    rolled = pltpu.roll(x, 64, 1)
    return jnp.where(lane < 64, -rolled, rolled)


def tile_sum(x):
    rows, cols = x.shape
    total = None
    for j in range(cols // 128):
        part = jnp.sum(x[:, 128 * j : 128 * j + 128].reshape(rows // 8, 8, 128), axis=0)
        total = part if total is None else total + part
    return total


def full_sum(tile):
    return jnp.sum(jnp.sum(tile, axis=0, keepdims=True), axis=1, keepdims=True)


def kernel(op_hbm, rec, sol, res, en, tail, xs, xc, u, wt, z, pb, fb, pf, ff, rzh, rzf, ryc, ryh, ryf,
           sbuf, rrow, rcol, rfreq, load_sem, send_sem, recv_sem):
    freq, row, col = lax.axis_index("freq"), lax.axis_index("row"), lax.axis_index("col")
    y, q = row // 2, row % 2

    source = op_hbm.reshape(2 * N, N)
    loads = [
        pltpu.make_async_copy(source.at[:, pl.ds(128 * j, 128)], en.at[j, pl.ds(0, 2 * N)], load_sem.at[j])
        for j in range(11)
    ]
    loads.append(pltpu.make_async_copy(source.at[:, pl.ds(1408, LAST)], tail, load_sem.at[11]))
    for c in loads:
        c.start()

    row_peers = [{"row": (row + k) % 8} for k in range(1, 8)]
    col_peers = [{"col": (col + k) % 8} for k in range(1, 8)]
    freq_peers = [{"freq": (freq + k) % 4} for k in range(1, 4)]
    barrier = pltpu.get_barrier_semaphore()
    for peer in row_peers + col_peers + freq_peers:
        pl.semaphore_signal(barrier, inc=1, device_id=peer, device_id_type=MESH)

    count = [0]
    sent = []

    def message(src, dst, peer):
        k = count[0]
        count[0] += 1
        copy = pltpu.make_async_remote_copy(
            src_ref=src, dst_ref=dst, send_sem=send_sem.at[k], recv_sem=recv_sem.at[k],
            device_id=peer, device_id_type=MESH)
        copy.start()
        sent.append(copy)
        return k

    def arrive(k, dst):
        pltpu.make_async_remote_copy(
            src_ref=dst, dst_ref=dst, send_sem=send_sem.at[k], recv_sem=recv_sem.at[k],
            device_id={"col": (col + 1) % 8}, device_id_type=MESH).wait_recv()

    def zrows(k, part=None):
        start = pl.multiple_of(ZC * ((col + k + 8) % 8), 64)
        if part is None:
            return pl.ds(start, ZC)
        return pl.ds(pl.multiple_of(start + part * (ZC // 2), 32), ZC // 2)

    z_up, z_down = {"col": (col + 1) % 8}, {"col": (col + 7) % 8}

    def z_phase(it, s):
        p, f = pf.at[it, s], ff.at[it, s]
        half, full = rzh.at[it, s], rzf.at[it, s]
        a = message(p.at[zrows(4, 0)], half.at[0], z_up)
        b = message(p.at[zrows(4, 1)], half.at[1], z_down)
        yield
        arrive(a, half.at[0])
        p[zrows(3, 0), :] += half[0]
        a = message(p.at[zrows(3)], full.at[0, 0], z_up)
        arrive(b, half.at[1])
        p[zrows(-3, 1), :] += half[1]
        b = message(p.at[zrows(-3)], full.at[1, 0], z_down)
        yield
        for step in range(2):
            arrive(a, full.at[0, step])
            p[zrows(2 - step), :] += full[0, step]
            a = message(p.at[zrows(2 - step)], full.at[0, step + 1], z_up)
            arrive(b, full.at[1, step])
            p[zrows(step - 2), :] += full[1, step]
            b = message(p.at[zrows(step - 2)], full.at[1, step + 1], z_down)
            yield
        arrive(a, full.at[0, 2])
        arrive(b, full.at[1, 2])
        f[zrows(0), :] = p[zrows(0), :] + full[0, 2] + full[1, 2]
        a = message(f.at[zrows(0)], f.at[zrows(0)], z_up)
        b = message(f.at[zrows(0)], f.at[zrows(0)], z_down)
        yield
        for step in range(1, 3):
            arrive(a, f.at[zrows(-step)])
            a = message(f.at[zrows(-step)], f.at[zrows(-step)], z_up)
            arrive(b, f.at[zrows(step)])
            b = message(f.at[zrows(step)], f.at[zrows(step)], z_down)
            yield
        arrive(a, f.at[zrows(-3)])
        a = message(f.at[zrows(-3, 0)], f.at[zrows(-3, 0)], z_up)
        arrive(b, f.at[zrows(3)])
        b = message(f.at[zrows(3, 1)], f.at[zrows(3, 1)], z_down)
        yield
        arrive(a, f.at[zrows(4, 0)])
        arrive(b, f.at[zrows(4, 1)])
        yield

    def yrows(k, part=None, core=None):
        owner = 4 * (q if core is None else core) + (y + k + 4) % 4
        start = pl.multiple_of(16 * owner, 16)
        if part is None:
            return pl.ds(start, 16)
        return pl.ds(pl.multiple_of(start + 8 * part, 8), 8)

    y_up, y_down = {"row": 2 * ((y + 1) % 4) + q}, {"row": 2 * ((y + 3) % 4) + q}
    twin = {"row": 2 * y + (1 - q)}
    mine, other = pl.ds(pl.multiple_of(64 * q, 64), 64), pl.ds(pl.multiple_of(64 * (1 - q), 64), 64)

    def y_phase(it, s):
        p, f = pb.at[it, s], fb.at[it, s]
        half, full = ryh.at[it, s], ryf.at[it, s]
        a = message(p.at[other], ryc.at[it, s], twin)
        yield
        arrive(a, ryc.at[it, s])
        p[mine, :] += ryc[it, s]
        a = message(p.at[yrows(2, 0)], half.at[0], y_up)
        b = message(p.at[yrows(2, 1)], half.at[1], y_down)
        yield
        arrive(a, half.at[0])
        p[yrows(1, 0), :] += half[0]
        a = message(p.at[yrows(1)], full.at[0], y_up)
        arrive(b, half.at[1])
        p[yrows(-1, 1), :] += half[1]
        b = message(p.at[yrows(-1)], full.at[1], y_down)
        yield
        arrive(a, full.at[0])
        arrive(b, full.at[1])
        f[yrows(0), :] = p[yrows(0), :] + full[0] + full[1]
        a = message(f.at[yrows(0)], f.at[yrows(0)], y_up)
        b = message(f.at[yrows(0)], f.at[yrows(0)], y_down)
        twins = [(message(f.at[yrows(0)], f.at[yrows(0)], twin), 0)]
        yield
        arrive(a, f.at[yrows(-1)])
        a = message(f.at[yrows(-1, 0)], f.at[yrows(-1, 0)], y_up)
        twins.append((message(f.at[yrows(-1)], f.at[yrows(-1)], twin), -1))
        arrive(b, f.at[yrows(1)])
        b = message(f.at[yrows(1, 1)], f.at[yrows(1, 1)], y_down)
        twins.append((message(f.at[yrows(1)], f.at[yrows(1)], twin), 1))
        yield
        arrive(a, f.at[yrows(2, 0)])
        arrive(b, f.at[yrows(2, 1)])
        twins.append((message(f.at[yrows(2)], f.at[yrows(2)], twin), 2))
        yield
        for k, place in twins:
            arrive(k, f.at[yrows(place, core=1 - q)])
        yield

    def exchange(n, tiles, out):
        rows = 8 * len(tiles)
        value = jnp.concatenate(tiles, axis=0) if len(tiles) > 1 else tiles[0]
        for stage, (slots, size, me, peers) in enumerate(
            ((rrow, 8, row, row_peers), (rcol, 8, col, col_peers), (rfreq, 4, freq, freq_peers))
        ):
            sbuf[n, stage, pl.ds(0, rows), :] = value
            slots[n, me, pl.ds(0, rows), :] = value
            keys = [
                message(sbuf.at[n, stage, pl.ds(0, rows)], slots.at[n, me, pl.ds(0, rows)], peer) for peer in peers
            ]
            yield
            for k, key in enumerate(keys):
                arrive(key, slots.at[n, (me + size - k - 1) % size, pl.ds(0, rows)])
            value = slots[n, 0, pl.ds(0, rows), :]
            for j in range(1, size):
                value = value + slots[n, j, pl.ds(0, rows), :]
        out.extend(full_sum(value[8 * i : 8 * i + 8]) for i in range(len(tiles)))
        yield

    def set_weights(s, value):
        xs[pl.ds(0, NP, 2), :] = value
        xs[pl.ds(1, NP, 2), :] = -turn(value)
        for b in range(24):
            wt[s, :, 128 * b : 128 * b + 128] = xs[128 * b : 128 * b + 128, :].T.astype(BF16)

    def adjoint(it, s, lo, hi):
        @pl.loop(lo, hi)
        def _(j):
            block = jnp.concatenate([en[2 * j], en[2 * j + 1]], axis=1)
            pb[it, s, :, pl.ds(pl.multiple_of(256 * j, 256), 256)] = dot(wt[s], block)

    def forward_chunk(it, s, k):
        c = (col + k) % 8
        rows = pl.ds(pl.multiple_of(2 * ZC * c, 128), 2 * ZC)
        xc[...] = dot(jnp.concatenate([en[j, rows, :] for j in range(12)], axis=1), z[s])
        pf[it, s, pl.ds(pl.multiple_of(ZC * c, 64), ZC), :] = xc[pl.ds(0, ZC, 2), :] + turn(xc[pl.ds(1, ZC, 2), :])

    def forward(it, s):
        forward_chunk(it, s, 4)
        yield
        for first, step in ((3, 2), (2, 4), (1, 6)):
            @pl.loop(0, 2)
            def _(i):
                forward_chunk(it, s, first + step * i)
            yield
        forward_chunk(it, s, 0)
        yield

    def own_z(ref, it, s):
        return ref[it, s, zrows(0), :]

    xs[pl.ds(0, 2 * N), :] = rec[...].astype(F32)
    xs[pl.ds(2 * N, 72), :] = jnp.zeros((72, 128), F32)
    lane = lax.broadcasted_iota(jnp.int32, (NP, 128), 1)
    re, im = xs[pl.ds(0, NP, 2), :], xs[pl.ds(1, NP, 2), :]
    u[0] = jnp.where(lane < 64, re, pltpu.roll(im, 64, 1))
    u[1] = jnp.where(lane < 64, pltpu.roll(re, 64, 1), im)
    set_weights(0, u[0])
    set_weights(1, u[1])
    own_u = [u[s, zrows(0), :] for s in range(2)]
    beta1_tile = tile_sum(own_u[0] * own_u[0]) + tile_sum(own_u[1] * own_u[1])
    for c in loads:
        c.wait()
    en[:, pl.ds(2 * N, 72), :] = jnp.zeros((12, 72, 128), BF16)
    en[11] = jnp.pad(tail[...], ((0, 72), (0, 128 - LAST)))

    adjoint(0, 0, 0, 6)
    pl.semaphore_wait(barrier, len(row_peers + col_peers + freq_peers))

    ra, rb = y_phase(0, 0), y_phase(0, 1)
    next(ra)
    adjoint(0, 1, 0, 6)
    next(ra)
    next(rb)
    next(ra)
    next(rb)
    next(ra)
    next(rb)
    next(ra)
    next(rb)
    own = [fb[0, s, yrows(0), :] for s in range(2)]
    norms = []
    x0 = exchange(0, [beta1_tile, tile_sum(own[0] * own[0]) + tile_sum(own[1] * own[1])], norms)
    next(x0)
    next(ra)
    next(rb)
    next(ra)

    def set_operand(s, value):
        for b in range(12):
            z[s, 128 * b : 128 * b + 128, :] = value(b).T.astype(BF16)

    def lanes(b):
        return pl.ds(128 * b, 128)

    set_operand(0, lambda b: fb[0, 0, :, lanes(b)])
    ma, za = forward(0, 0), z_phase(0, 0)
    next(ma)
    next(za)
    next(rb)
    next(ma)
    next(za)
    next(rb)
    next(x0)
    next(ma)
    next(za)
    set_operand(1, lambda b: fb[0, 1, :, lanes(b)])
    next(ma)
    next(za)
    next(x0)
    next(ma)
    mb, zb = forward(0, 1), z_phase(0, 1)
    next(mb)
    next(zb)
    next(za)
    next(mb)
    next(zb)
    next(za)
    next(x0)
    beta1 = jnp.sqrt(norms[0] + EPS)
    alpha1 = jnp.sqrt(norms[1] / (beta1 * beta1) + EPS)
    k1 = 1.0 / (beta1 * alpha1)
    k2 = alpha1 / beta1
    next(mb)
    next(zb)
    next(za)
    next(mb)
    next(zb)
    next(za)
    next(mb)
    next(za)

    def update(s):
        return ff[0, s] * k1 - u[s] * k2

    set_weights(0, update(0))
    next(zb)
    own_update = [own_z(ff, 0, s) * k1 - own_u[s] * k2 for s in range(2)]
    x1 = exchange(1, [tile_sum(own_update[0] * own_update[0]) + tile_sum(own_update[1] * own_update[1])], norms)
    next(x1)
    adjoint(1, 0, 0, 3)
    next(zb)
    adjoint(1, 0, 3, 6)
    ra, rb = y_phase(1, 0), y_phase(1, 1)
    next(ra)
    next(zb)
    next(ra)
    next(x1)
    next(zb)
    next(ra)
    next(x1)
    next(zb)
    set_weights(1, update(1))
    next(ra)
    adjoint(1, 1, 0, 3)
    next(ra)
    adjoint(1, 1, 3, 6)
    next(rb)
    next(x1)
    beta2 = jnp.sqrt(norms[2] + EPS)
    ib2 = 1.0 / beta2
    k3 = beta2 * k1
    next(ra)
    next(rb)
    next(ra)
    set_operand(0, lambda b: fb[1, 0, :, lanes(b)] * ib2 - fb[0, 0, :, lanes(b)] * k3)
    ma, za = forward(1, 0), z_phase(1, 0)
    next(ma)
    next(za)
    next(rb)
    next(ma)
    next(za)
    next(rb)
    own = [fb[1, s, yrows(0), :] * ib2 - fb[0, s, yrows(0), :] * k3 for s in range(2)]
    x2 = exchange(2, [tile_sum(own[0] * own[0]) + tile_sum(own[1] * own[1])], norms)
    next(x2)
    next(ma)
    next(za)
    next(rb)
    next(ma)
    next(za)
    next(rb)
    next(x2)
    next(ma)
    next(rb)
    set_operand(1, lambda b: fb[1, 1, :, lanes(b)] * ib2 - fb[0, 1, :, lanes(b)] * k3)
    mb, zb = forward(1, 1), z_phase(1, 1)
    next(mb)
    next(zb)
    next(za)
    next(x2)
    next(mb)
    next(zb)
    next(za)
    next(x2)
    alpha2 = jnp.sqrt(norms[3] + EPS)
    ia2 = 1.0 / alpha2
    next(mb)
    next(zb)
    next(za)
    next(mb)
    next(zb)
    next(za)
    next(mb)
    next(za)
    next(zb)
    own_last = [own_z(ff, 1, s) * ia2 - own_update[s] * (alpha2 * ib2) for s in range(2)]
    x3 = exchange(3, [tile_sum(own_last[0] * own_last[0]) + tile_sum(own_last[1] * own_last[1])], norms)
    next(x3)
    next(zb)
    next(x3)
    next(zb)
    next(x3)
    next(zb)
    next(x3)
    beta3 = jnp.sqrt(norms[4] + EPS)
    rho1 = jnp.sqrt(alpha1 * alpha1 + beta2 * beta2)
    cos1, sin1 = alpha1 / rho1, beta2 / rho1
    gain1 = cos1 * beta1 / rho1
    ratio = sin1 * alpha2 / rho1
    rho_bar = -cos1 * alpha2
    rho2 = jnp.sqrt(rho_bar * rho_bar + beta3 * beta3)
    gain2 = rho_bar / rho2 * (sin1 * beta1) / rho2
    first, second = (gain1 - gain2 * ratio) * k1, gain2 * ia2
    second_a, second_b = second * ib2, first - second * k3

    for part in range(2):
        for b in range(12):
            rows = pl.ds(64 * part, 64)
            block = jnp.concatenate(
                [fb[1, s, rows, lanes(b)] * second_a + fb[0, s, rows, lanes(b)] * second_b for s in range(2)], axis=0)
            size = 128 if b < 11 else LAST
            sol[pl.ds(256 * b + part, size, 2), :] = block.T[:size]
    next(zb)
    lane = lax.broadcasted_iota(jnp.int32, (N, 128), 1)
    out = [
        u[s, pl.ds(0, N), :] - ff[0, s, pl.ds(0, N), :] * first - ff[1, s, pl.ds(0, N), :] * second for s in range(2)
    ]
    res[pl.ds(0, N, 2), :] = jnp.where(lane < 64, out[0], pltpu.roll(out[1], 64, 1))
    res[pl.ds(1, N, 2), :] = jnp.where(lane < 64, pltpu.roll(out[0], 64, 1), out[1])

    for copy in sent:
        copy.wait_send()


def shards(operator, recorded):
    op = jnp.transpose(operator[0], (1, 0, 2))
    rec = jnp.transpose(recorded[0], (1, 0, 2)).reshape(2 * N, 128)
    vmem = pl.BlockSpec(memory_space=pltpu.VMEM)
    out = jax.ShapeDtypeStruct((2 * N, 128), F32)
    sol, res = pl.pallas_call(
        kernel,
        out_shape=[out, out],
        in_specs=[pl.BlockSpec(memory_space=pl.ANY), vmem],
        out_specs=[vmem, vmem],
        scratch_shapes=[
            pltpu.VMEM((12, 2 * NP, 128), BF16),
            pltpu.VMEM((2 * N, LAST), BF16),
            pltpu.VMEM((2 * NP, 128), F32),
            pltpu.VMEM((2 * ZC, 128), F32),
            pltpu.VMEM((2, NP, 128), F32),
            pltpu.VMEM((2, 128, 2 * NP), BF16),
            pltpu.VMEM((2, NP, 128), BF16),
            pltpu.VMEM((2, 2, 128, NP), F32),
            pltpu.VMEM((2, 2, 128, NP), F32),
            pltpu.VMEM((2, 2, NP, 128), F32),
            pltpu.VMEM((2, 2, NP, 128), F32),
            pltpu.VMEM((2, 2, 2, ZC // 2, 128), F32),
            pltpu.VMEM((2, 2, 2, 3, ZC, 128), F32),
            pltpu.VMEM((2, 2, 64, NP), F32),
            pltpu.VMEM((2, 2, 2, 8, NP), F32),
            pltpu.VMEM((2, 2, 2, 16, NP), F32),
            pltpu.VMEM((4, 3, 16, 128), F32),
            pltpu.VMEM((4, 8, 16, 128), F32),
            pltpu.VMEM((4, 8, 16, 128), F32),
            pltpu.VMEM((4, 4, 16, 128), F32),
            pltpu.SemaphoreType.DMA((12,)),
            pltpu.SemaphoreType.DMA((MESSAGES,)),
            pltpu.SemaphoreType.DMA((MESSAGES,)),
        ],
        compiler_params=pltpu.CompilerParams(
            collective_id=0, has_side_effects=True, vmem_limit_bytes=60 * 2**20),
        cost_estimate=pl.CostEstimate(flops=9_437_184_000, bytes_accessed=13_000_000, transcendentals=0),
    )(op, rec)
    return tuple(jnp.transpose(o.reshape(N, 2, 128), (1, 0, 2))[None] for o in (sol, res))


def solution(mesh):
    in_specs = (P("freq", None, "row", "col"), P("freq", None, "row", None))
    out_specs = (P("freq", None, "col", None), P("freq", None, "row", None))
    return jax.shard_map(shards, mesh=mesh, in_specs=in_specs, out_specs=out_specs, check_vma=False)
```

```python
import math

import jax
import jax.numpy as jnp
from jax import lax
from jax.experimental import pallas as pl
from jax.experimental.pallas import tpu as pltpu
from jax.sharding import PartitionSpec as P

MESH = pl.DeviceIdType.MESH
EPS = 1e-06
N = 1500
NP = 1536
LAST = N - 11 * 128
ZC = NP // 8
F32, BF16 = jnp.float32, jnp.bfloat16
MESSAGES = 304
SUBS = 2
Y_SUBS = 2
Y_DIRECT = False
LAT = 2.3
RS_SHORT = False
AG_SHORT = False


def dot(a, b):
    return lax.dot_general(a, b, (((1,), (0,)), ((), ())), preferred_element_type=F32)


def turn(x):
    lane = lax.broadcasted_iota(jnp.int32, x.shape, 1)
    rolled = pltpu.roll(x, 64, 1)
    return jnp.where(lane < 64, -rolled, rolled)


def tile_sum(x):
    rows, cols = x.shape
    total = None
    for j in range(cols // 128):
        part = jnp.sum(x[:, 128 * j : 128 * j + 128].reshape(rows // 8, 8, 128), axis=0)
        total = part if total is None else total + part
    return total


def full_sum(tile):
    return jnp.sum(jnp.sum(tile, axis=0, keepdims=True), axis=1, keepdims=True)


class Plan:
    def __init__(self):
        self.now, self.links, self.due, self.marks = 0.0, {}, [], set()

    def send(self, links, occupied, latency):
        self.now += 0.05
        start = max([self.now] + [self.links.get(link, 0.0) for link in links])
        for link in links:
            self.links[link] = start + occupied
        self.due.append(start + occupied + latency)
        return len(self.due) - 1

    def run(self, streams):
        waiting = [(stream, next(stream)) for stream in streams]
        while waiting:
            best = None
            for place, (stream, (keys, marks)) in enumerate(waiting):
                if all(mark in self.marks for mark in marks):
                    ready = max([self.now] + [self.due[k] for k in keys])
                    if best is None or ready < best[0]:
                        best = (ready, place)
            self.now, place = best
            stream = waiting[place][0]
            try:
                waiting[place] = (stream, next(stream))
            except StopIteration:
                del waiting[place]


def kernel(op_hbm, rec, sol, res, en, tail, xs, xc, u, wt, z, pb, fb, pf, ff, rzh, rzf, ryc, ryh, ryf,
           sbuf, rrow, rcol, rfreq, load_sem, send_sem, recv_sem):
    freq, row, col = lax.axis_index("freq"), lax.axis_index("row"), lax.axis_index("col")
    y, q = row // 2, row % 2
    plan = Plan()

    source = op_hbm.reshape(2 * N, N)
    loads = [
        pltpu.make_async_copy(source.at[:, pl.ds(128 * j, 128)], en.at[j, pl.ds(0, 2 * N)], load_sem.at[j])
        for j in range(11)
    ]
    loads.append(pltpu.make_async_copy(source.at[:, pl.ds(1408, LAST)], tail, load_sem.at[11]))
    for c in loads:
        c.start()

    row_peers = [{"row": (row + k) % 8} for k in range(1, 8)]
    col_peers = [{"col": (col + k) % 8} for k in range(1, 8)]
    freq_peers = [{"freq": (freq + k) % 4} for k in range(1, 4)]
    peers = row_peers + col_peers + freq_peers
    barrier = pltpu.get_barrier_semaphore()
    for peer in peers:
        pl.semaphore_signal(barrier, inc=1, device_id=peer, device_id_type=MESH)

    sent = []

    def message(src, dst, peer, links=(), hops=1, latency=LAT):
        if not sent:
            pl.semaphore_wait(barrier, len(peers))
        size = 4 * math.prod(src.shape)
        k = plan.send(links, hops * size * 2e-5 if links else size * 1.5e-6, latency + 0.6 * (hops - 1))
        copy = pltpu.make_async_remote_copy(
            src_ref=src, dst_ref=dst, send_sem=send_sem.at[k], recv_sem=recv_sem.at[k],
            device_id=peer, device_id_type=MESH)
        copy.start()
        sent.append(copy)
        return k

    def arrive(k, dst):
        pltpu.make_async_remote_copy(
            src_ref=dst, dst_ref=dst, send_sem=send_sem.at[k], recv_sem=recv_sem.at[k],
            device_id={"col": (col + 1) % 8}, device_id_type=MESH).wait_recv()

    def mark(*name):
        plan.marks.add(name)

    size = ZC // SUBS

    def zrows(k, h, part=None):
        start = ZC * ((col + k + 8) % 8) + size * h
        if part is None:
            return pl.ds(pl.multiple_of(start, 16), size)
        return pl.ds(pl.multiple_of(start + part * (size // 2), 16), size // 2)

    def z_peer(step):
        return {"col": (col + 8 + step) % 8}

    def z_phase(it, s, h):
        p, f = pf.at[it, s], ff.at[it, s]
        half, full = rzh.at[it, s, h], rzf.at[it, s, h]
        signs = (1, -1)

        def go(src, dst, sign, hops=1):
            return message(src, dst, z_peer(sign * hops), (("z", sign),), hops)

        yield [], [("pf", it, s, 0)]
        if RS_SHORT:
            far = [go(p.at[zrows(4, h, d)], half.at[d], sign, 2) for d, sign in enumerate(signs)]
        else:
            far = [go(p.at[zrows(4, h, d)], half.at[d], sign) for d, sign in enumerate(signs)]
        keys = [None, None]
        for step in (3, 2, 1):
            for d, sign in enumerate(signs):
                at = 2 if RS_SHORT else 3
                needs = ([] if step == 3 else [keys[d]]) + ([far[d]] if step == at else [])
                yield needs, [("pf", it, s, 4 - step)]
                if step < 3:
                    arrive(keys[d], full.at[d, 2 - step])
                    p[zrows(sign * step, h), :] += full[d, 2 - step]
                if step == at:
                    arrive(far[d], half.at[d])
                    p[zrows(sign * step, h, d), :] += half[d]
                keys[d] = go(p.at[zrows(sign * step, h)], full.at[d, 3 - step], sign)
        yield keys, [("pf", it, s, 4)]
        for d in range(2):
            arrive(keys[d], full.at[d, 2])
        f[zrows(0, h), :] = p[zrows(0, h), :] + full[0, 2] + full[1, 2]
        mark("own_z", it, s, h)
        here = f.at[zrows(0, h)]
        keys = [go(here, here, sign) for sign in signs]
        for step in (1, 2, 3):
            for d, sign in enumerate(signs):
                yield [keys[d]], []
                block = f.at[zrows(-sign * step, h)]
                arrive(keys[d], block)
                if step == 2 and AG_SHORT:
                    part = f.at[zrows(-sign * step, h, d)]
                    far[d] = go(part, part, sign, 2)
                if step < 3:
                    keys[d] = go(block, block, sign)
                elif not AG_SHORT:
                    part = f.at[zrows(-sign * step, h, d)]
                    far[d] = go(part, part, sign)
        yield far, []
        for d in range(2):
            arrive(far[d], f.at[zrows(4, h, d)])
        mark("ff", it, s, h)

    def yrows(k, core=None, part=None):
        owner = 4 * (q if core is None else core) + (y + k + 4) % 4
        if part is None:
            return pl.ds(pl.multiple_of(16 * owner, 16), 16)
        return pl.ds(pl.multiple_of(16 * owner + 8 * part, 8), 8)

    y_links = {1: (("y", 1),), 2: (("y", 1), ("y", -1)), 3: (("y", -1),)}
    twin = {"row": 2 * y + (1 - q)}
    mine, other = pl.ds(pl.multiple_of(64 * q, 64), 64), pl.ds(pl.multiple_of(64 * (1 - q), 64), 64)
    width = NP // Y_SUBS

    def y_phase(it, s, h):
        across = pl.ds(width * h, width)
        p, f = pb.at[it, s], fb.at[it, s]
        core_half, half, full = ryc.at[it, s, h], ryh.at[it, s, h], ryf.at[it, s, h]
        signs = (1, -1)

        def go(src, dst, k):
            return message(src, dst, {"row": 2 * ((y + k) % 4) + q}, y_links[k], 1, LAT + (0.6 if k == 2 else 0.0))

        def pass_on(k):
            block = f.at[yrows(k), across]
            return message(block, block, twin, (), 1, 0.9), k

        yield [], [("pb", it, s, part) for part in range(3) if 512 * part < width * (h + 1)]
        a = message(p.at[other, across], core_half, twin, (), 1, 0.9)
        yield [a], []
        arrive(a, core_half)
        p[mine, across] += core_half[...]
        if Y_DIRECT:
            keys = {k: go(p.at[yrows(k), across], full.at[k - 1], k) for k in (2, 1, 3)}
            yield list(keys.values()), []
            total = p[yrows(0), across]
            for k in (1, 3, 2):
                arrive(keys[k], full.at[k - 1])
                total = total + full[k - 1]
        else:
            far = [go(p.at[yrows(2, None, d), across], half.at[d], sign % 4) for d, sign in enumerate(signs)]
            keys = [None, None]
            for d, sign in enumerate(signs):
                yield [far[d]], []
                arrive(far[d], half.at[d])
                p[yrows(sign, None, d), across] += half[d]
                keys[d] = go(p.at[yrows(sign), across], full.at[d], sign % 4)
            yield keys, []
            total = p[yrows(0), across]
            for d in range(2):
                arrive(keys[d], full.at[d])
                total = total + full[d]
        f[yrows(0), across] = total
        mark("own_y", it, s, h)
        here = f.at[yrows(0), across]
        if Y_DIRECT:
            keys = {k: go(here, here, k) for k in (2, 1, 3)}
            twins = [pass_on(0)]
            for k in (1, 3, 2):
                yield [keys[k]], []
                arrive(keys[k], f.at[yrows(-k), across])
                twins.append(pass_on(-k))
        else:
            keys = [go(here, here, sign % 4) for sign in signs]
            twins = [pass_on(0)]
            for d, sign in enumerate(signs):
                yield [keys[d]], []
                arrive(keys[d], f.at[yrows(-sign), across])
                part = f.at[yrows(-sign, None, d), across]
                far[d] = go(part, part, sign % 4)
                twins.append(pass_on(-sign))
            yield far, []
            for d in range(2):
                arrive(far[d], f.at[yrows(2, None, d), across])
            twins.append(pass_on(2))
        yield [k for k, _ in twins], []
        for k, place in twins:
            arrive(k, f.at[yrows(place, core=1 - q), across])
        mark("fb", it, s, h)

    norms = {}

    def exchange(n, names, needs, tiles):
        yield [], needs
        value = tiles()
        rows = 8 * len(names)
        for stage, (slots, size, me, group, hops) in enumerate(
            ((rrow, 8, row, row_peers, 2), (rcol, 8, col, col_peers, 4), (rfreq, 4, freq, freq_peers, 2))
        ):
            sbuf[n, stage, pl.ds(0, rows), :] = value
            slots[n, me, pl.ds(0, rows), :] = value
            order = sorted(range(size - 1), key=lambda k: abs(2 * k + 2 - size))
            keys = {
                k: message(sbuf.at[n, stage, pl.ds(0, rows)], slots.at[n, me, pl.ds(0, rows)], group[k], (), hops)
                for k in order
            }
            yield list(keys.values()), []
            for k, key in keys.items():
                arrive(key, slots.at[n, (me + size - k - 1) % size, pl.ds(0, rows)])
            value = slots[n, 0, pl.ds(0, rows), :]
            for j in range(1, size):
                value = value + slots[n, j, pl.ds(0, rows), :]
        for i, name in enumerate(names):
            norms[name] = full_sum(value[8 * i : 8 * i + 8])
        mark("x", n)

    def lanes(b):
        return pl.ds(128 * b, 128)

    def set_weights(s, value):
        xs[pl.ds(0, NP, 2), :] = value
        xs[pl.ds(1, NP, 2), :] = -turn(value)
        for b in range(24):
            wt[s, :, 128 * b : 128 * b + 128] = xs[128 * b : 128 * b + 128, :].T.astype(BF16)
        plan.now += 0.4

    loaded = []

    def fetched(part):
        for j in range(4 * part, 4 * part + 4):
            loads[j].wait()
            if j < 11:
                en[j, pl.ds(2 * N, 72), :] = jnp.zeros((72, 128), BF16)
            else:
                en[11] = jnp.pad(tail[...], ((0, 72), (0, 128 - LAST)))
        loaded.append(part)

    def adjoint(it, s):
        for part in range(3):
            yield [], []
            if part not in loaded:
                fetched(part)
            block = jnp.concatenate([en[4 * part + j] for j in range(4)], axis=1)
            pb[it, s, :, 512 * part : 512 * part + 512] = dot(wt[s], block)
            plan.now += 0.5
            mark("pb", it, s, part)

    def set_operand(s, value):
        for b in range(12):
            z[s, 128 * b : 128 * b + 128, :] = value(b).T.astype(BF16)
        plan.now += 0.2

    def forward_chunk(it, s, k, i):
        c = (col + k) % 8
        rows = pl.ds(pl.multiple_of(2 * ZC * c, 128), 2 * ZC)
        xc[i] = dot(jnp.concatenate([en[j, rows, :] for j in range(12)], axis=1), z[s])
        even, odd = xc[i, pl.ds(0, ZC, 2), :], xc[i, pl.ds(1, ZC, 2), :]
        pf[it, s, pl.ds(pl.multiple_of(ZC * c, 64), ZC), :] = even + turn(odd)

    def forward(it, s):
        for group, (first, step, count) in enumerate(((4, 0, 1), (3, 2, 2), (2, 4, 2), (1, 6, 2), (0, 0, 1))):
            yield [], []
            for i in range(count):
                forward_chunk(it, s, first + step * i, i)
            plan.now += 0.4 * count
            mark("pf", it, s, group)

    xs[pl.ds(0, 2 * N), :] = rec[...].astype(F32)
    xs[pl.ds(2 * N, 72), :] = jnp.zeros((72, 128), F32)
    lane = lax.broadcasted_iota(jnp.int32, (NP, 128), 1)
    re, im = xs[pl.ds(0, NP, 2), :], xs[pl.ds(1, NP, 2), :]
    u[0] = jnp.where(lane < 64, re, pltpu.roll(im, 64, 1))
    u[1] = jnp.where(lane < 64, pltpu.roll(re, 64, 1), im)
    set_weights(0, u[0])
    set_weights(1, u[1])

    def own_rows(ref):
        return ref[pl.ds(pl.multiple_of(ZC * col, 64), ZC), :]

    def square_sum(values):
        return tile_sum(values[0] * values[0]) + tile_sum(values[1] * values[1])

    val = {}

    def tiles0():
        own = [fb[0, s, yrows(0), :] for s in range(2)]
        return jnp.concatenate([square_sum([own_rows(u.at[s]) for s in range(2)]), square_sum(own)], axis=0)

    def after0():
        if "k1" not in val:
            val["beta1"] = jnp.sqrt(norms["beta1"] + EPS)
            val["alpha1"] = jnp.sqrt(norms["alpha1"] / (val["beta1"] * val["beta1"]) + EPS)
            val["k1"] = 1.0 / (val["beta1"] * val["alpha1"])
            val["k2"] = val["alpha1"] / val["beta1"]

    def own_update(s):
        after0()
        return own_rows(ff.at[0, s]) * val["k1"] - own_rows(u.at[s]) * val["k2"]

    def tiles1():
        return square_sum([own_update(s) for s in range(2)])

    def after1():
        if "ib2" not in val:
            val["beta2"] = jnp.sqrt(norms["beta2"] + EPS)
            val["ib2"] = 1.0 / val["beta2"]
            val["k3"] = val["beta2"] * val["k1"]

    def tiles2():
        after1()
        return square_sum([fb[1, s, yrows(0), :] * val["ib2"] - fb[0, s, yrows(0), :] * val["k3"] for s in range(2)])

    def after2():
        if "ia2" not in val:
            val["alpha2"] = jnp.sqrt(norms["alpha2"] + EPS)
            val["ia2"] = 1.0 / val["alpha2"]

    def tiles3():
        after2()
        ratio = val["alpha2"] * val["ib2"]
        return square_sum([own_rows(ff.at[1, s]) * val["ia2"] - own_update(s) * ratio for s in range(2)])

    def work(s):
        yield from adjoint(0, s)
        yield [], [("fb", 0, s, h) for h in range(Y_SUBS)]
        set_operand(s, lambda b: fb[0, s, :, lanes(b)])
        yield from forward(0, s)
        yield [], [("x", 0)] + [("ff", 0, s, h) for h in range(SUBS)]
        after0()
        set_weights(s, ff[0, s] * val["k1"] - u[s] * val["k2"])
        yield from adjoint(1, s)
        yield [], [("x", 1)] + [("fb", 1, s, h) for h in range(Y_SUBS)]
        after1()
        set_operand(s, lambda b: fb[1, s, :, lanes(b)] * val["ib2"] - fb[0, s, :, lanes(b)] * val["k3"])
        yield from forward(1, s)

    def finish():
        yield [], [("x", 3)]
        beta1, alpha1, beta2, alpha2 = val["beta1"], val["alpha1"], val["beta2"], val["alpha2"]
        beta3 = jnp.sqrt(norms["beta3"] + EPS)
        rho1 = jnp.sqrt(alpha1 * alpha1 + beta2 * beta2)
        cos1, sin1 = alpha1 / rho1, beta2 / rho1
        gain1 = cos1 * beta1 / rho1
        ratio = sin1 * alpha2 / rho1
        rho_bar = -cos1 * alpha2
        rho2 = jnp.sqrt(rho_bar * rho_bar + beta3 * beta3)
        gain2 = rho_bar / rho2 * (sin1 * beta1) / rho2
        first, second = (gain1 - gain2 * ratio) * val["k1"], gain2 * val["ia2"]
        second_a, second_b = second * val["ib2"], first - second * val["k3"]
        for part in range(2):
            for b in range(12):
                rows = pl.ds(64 * part, 64)
                block = jnp.concatenate(
                    [fb[1, s, rows, lanes(b)] * second_a + fb[0, s, rows, lanes(b)] * second_b for s in range(2)], axis=0)
                length = 128 if b < 11 else LAST
                sol[pl.ds(256 * b + part, length, 2), :] = block.T[:length]
        plan.now += 1.0
        yield [], [("ff", 1, s, h) for s in range(2) for h in range(SUBS)]
        lane = lax.broadcasted_iota(jnp.int32, (N, 128), 1)
        out = [
            u[s, pl.ds(0, N), :] - ff[0, s, pl.ds(0, N), :] * first - ff[1, s, pl.ds(0, N), :] * second
            for s in range(2)
        ]
        res[pl.ds(0, N, 2), :] = jnp.where(lane < 64, out[0], pltpu.roll(out[1], 64, 1))
        res[pl.ds(1, N, 2), :] = jnp.where(lane < 64, pltpu.roll(out[0], 64, 1), out[1])
        plan.now += 0.5

    both = [(s, h) for s in range(2) for h in range(SUBS)]
    both_y = [(s, h) for s in range(2) for h in range(Y_SUBS)]
    streams = [z_phase(it, s, h) for it in range(2) for s, h in both]
    streams += [y_phase(it, s, h) for it in range(2) for s, h in both_y]
    streams.append(exchange(0, ("beta1", "alpha1"), [("own_y", 0, s, h) for s, h in both_y], tiles0))
    streams.append(exchange(1, ("beta2",), [("x", 0)] + [("own_z", 0, s, h) for s, h in both], tiles1))
    streams.append(exchange(2, ("alpha2",), [("x", 1)] + [("own_y", 1, s, h) for s, h in both_y], tiles2))
    streams.append(exchange(3, ("beta3",), [("x", 2)] + [("own_z", 1, s, h) for s, h in both], tiles3))
    streams += [work(0), work(1), finish()]
    plan.run(streams)
    assert len(sent) <= MESSAGES
    for copy in sent:
        copy.wait_send()


def shards(operator, recorded):
    op = jnp.transpose(operator[0], (1, 0, 2))
    rec = jnp.transpose(recorded[0], (1, 0, 2)).reshape(2 * N, 128)
    vmem = pl.BlockSpec(memory_space=pltpu.VMEM)
    out = jax.ShapeDtypeStruct((2 * N, 128), F32)
    sol, res = pl.pallas_call(
        kernel,
        out_shape=[out, out],
        in_specs=[pl.BlockSpec(memory_space=pl.ANY), vmem],
        out_specs=[vmem, vmem],
        scratch_shapes=[
            pltpu.VMEM((12, 2 * NP, 128), BF16),
            pltpu.VMEM((2 * N, LAST), BF16),
            pltpu.VMEM((2 * NP, 128), F32),
            pltpu.VMEM((2, 2 * ZC, 128), F32),
            pltpu.VMEM((2, NP, 128), F32),
            pltpu.VMEM((2, 128, 2 * NP), BF16),
            pltpu.VMEM((2, NP, 128), BF16),
            pltpu.VMEM((2, 2, 128, NP), F32),
            pltpu.VMEM((2, 2, 128, NP), F32),
            pltpu.VMEM((2, 2, NP, 128), F32),
            pltpu.VMEM((2, 2, NP, 128), F32),
            pltpu.VMEM((2, 2, SUBS, 2, ZC // SUBS // 2, 128), F32),
            pltpu.VMEM((2, 2, SUBS, 2, 3, ZC // SUBS, 128), F32),
            pltpu.VMEM((2, 2, Y_SUBS, 64, NP // Y_SUBS), F32),
            pltpu.VMEM((2, 2, Y_SUBS, 2, 8, NP // Y_SUBS), F32),
            pltpu.VMEM((2, 2, Y_SUBS, 3, 16, NP // Y_SUBS), F32),
            pltpu.VMEM((4, 3, 16, 128), F32),
            pltpu.VMEM((4, 8, 16, 128), F32),
            pltpu.VMEM((4, 8, 16, 128), F32),
            pltpu.VMEM((4, 4, 16, 128), F32),
            pltpu.SemaphoreType.DMA((12,)),
            pltpu.SemaphoreType.DMA((MESSAGES,)),
            pltpu.SemaphoreType.DMA((MESSAGES,)),
        ],
        compiler_params=pltpu.CompilerParams(
            collective_id=0, has_side_effects=True, vmem_limit_bytes=48 * 2**20),
        cost_estimate=pl.CostEstimate(flops=9_437_184_000, bytes_accessed=13_000_000, transcendentals=0),
    )(op, rec)
    return tuple(jnp.transpose(o.reshape(N, 2, 128), (1, 0, 2))[None] for o in (sol, res))


def solution(mesh):
    in_specs = (P("freq", None, "row", "col"), P("freq", None, "row", None))
    out_specs = (P("freq", None, "col", None), P("freq", None, "row", None))
    return jax.shard_map(shards, mesh=mesh, in_specs=in_specs, out_specs=out_specs, check_vma=False)
```

```python
import math

import jax
import jax.numpy as jnp
from jax import lax
from jax.experimental import pallas as pl
from jax.experimental.pallas import tpu as pltpu
from jax.sharding import PartitionSpec as P

MESH = pl.DeviceIdType.MESH
EPS = 1e-06
N = 1500
NP = 1536
LAST = N - 11 * 128
ZC = NP // 8
F32, BF16 = jnp.float32, jnp.bfloat16
MESSAGES = 304
SUBS = 2
Y_SUBS = 2
Y_DIRECT = False
LAT = 2.8
X_LAT = 3.6
BEHIND = 64
RS_SHORT = True
AG_SHORT = False


def dot(a, b):
    return lax.dot_general(a, b, (((1,), (0,)), ((), ())), preferred_element_type=F32)


def turn(x):
    lane = lax.broadcasted_iota(jnp.int32, x.shape, 1)
    rolled = pltpu.roll(x, 64, 1)
    return jnp.where(lane < 64, -rolled, rolled)


def tile_sum(x):
    rows, cols = x.shape
    total = None
    for j in range(cols // 128):
        part = jnp.sum(x[:, 128 * j : 128 * j + 128].reshape(rows // 8, 8, 128), axis=0)
        total = part if total is None else total + part
    return total


def full_sum(tile):
    return jnp.sum(jnp.sum(tile, axis=0, keepdims=True), axis=1, keepdims=True)


class Plan:
    def __init__(self):
        self.now, self.links, self.due, self.marks = 0.0, {}, [], set()

    def send(self, links, occupied, latency):
        self.now += 0.05
        start = max([self.now] + [self.links.get(link, 0.0) for link in links])
        for link in links:
            self.links[link] = start + occupied
        self.due.append(start + occupied + latency)
        return len(self.due) - 1

    def run(self, streams):
        waiting = [(stream, next(stream)) for stream in streams]
        while waiting:
            best = None
            for place, (stream, (keys, marks)) in enumerate(waiting):
                if all(mark in self.marks for mark in marks):
                    ready = max([self.now] + [self.due[k] for k in keys])
                    if best is None or ready < best[0]:
                        best = (ready, place)
            self.now, place = best
            stream = waiting[place][0]
            try:
                waiting[place] = (stream, next(stream))
            except StopIteration:
                del waiting[place]


def kernel(op_hbm, rec_hbm, sol, res, rec, en, tail, xs, xc, u, wt, z, pb, fb, pf, ff, rzh, rzf, ryc, ryh, ryf,
           sbuf, rrow, rcol, rfreq, load_sem, send_sem, recv_sem):
    freq, row, col = lax.axis_index("freq"), lax.axis_index("row"), lax.axis_index("col")
    y, q = row // 2, row % 2
    plan = Plan()

    source = op_hbm.reshape(2 * N, N)
    loads = [
        pltpu.make_async_copy(source.at[:, pl.ds(128 * j, 128)], en.at[j, pl.ds(0, 2 * N)], load_sem.at[j])
        for j in range(11)
    ]
    loads.append(pltpu.make_async_copy(source.at[:, pl.ds(1408, LAST)], tail, load_sem.at[11]))
    recorded = pltpu.make_async_copy(rec_hbm, rec, load_sem.at[12])
    recorded.start()
    for c in loads:
        c.start()

    row_peers = [{"row": (row + k) % 8} for k in range(1, 8)]
    col_peers = [{"col": (col + k) % 8} for k in range(1, 8)]
    freq_peers = [{"freq": (freq + k) % 4} for k in range(1, 4)]
    peers = row_peers + col_peers + freq_peers
    barrier = pltpu.get_barrier_semaphore()
    for peer in peers:
        pl.semaphore_signal(barrier, inc=1, device_id=peer, device_id_type=MESH)

    sent = []

    def message(src, dst, peer, links=(), hops=1, latency=LAT):
        if not sent:
            pl.semaphore_wait(barrier, len(peers))
        size = 4 * math.prod(src.shape)
        k = plan.send(links, hops * size * 2e-5 if links else size * 1.5e-6, latency + 0.6 * (hops - 1))
        copy = pltpu.make_async_remote_copy(
            src_ref=src, dst_ref=dst, send_sem=send_sem.at[k], recv_sem=recv_sem.at[k],
            device_id=peer, device_id_type=MESH)
        copy.start()
        sent.append(copy)
        if len(sent) > BEHIND:
            sent[-1 - BEHIND].wait_send()
        return k

    def arrive(k, dst):
        pltpu.make_async_remote_copy(
            src_ref=dst, dst_ref=dst, send_sem=send_sem.at[k], recv_sem=recv_sem.at[k],
            device_id={"col": (col + 1) % 8}, device_id_type=MESH).wait_recv()

    def mark(*name):
        plan.marks.add(name)

    size = ZC // SUBS

    def zrows(k, h, part=None):
        start = ZC * ((col + k + 8) % 8) + size * h
        if part is None:
            return pl.ds(pl.multiple_of(start, 16), size)
        return pl.ds(pl.multiple_of(start + part * (size // 2), 16), size // 2)

    def z_peer(step):
        return {"col": (col + 8 + step) % 8}

    def z_phase(it, s, h):
        p, f = pf.at[it, s], ff.at[it, s]
        half, full = rzh.at[it, s, h], rzf.at[it, s, h]
        signs = (1, -1)

        def go(src, dst, sign, hops=1):
            return message(src, dst, z_peer(sign * hops), (("z", sign),), hops)

        yield [], [("pf", it, s, 0)]
        if RS_SHORT:
            far = [go(p.at[zrows(4, h, d)], half.at[d], sign, 2) for d, sign in enumerate(signs)]
        else:
            far = [go(p.at[zrows(4, h, d)], half.at[d], sign) for d, sign in enumerate(signs)]
        keys = [None, None]
        for step in (3, 2, 1):
            for d, sign in enumerate(signs):
                at = 2 if RS_SHORT else 3
                needs = ([] if step == 3 else [keys[d]]) + ([far[d]] if step == at else [])
                yield needs, [("pf", it, s, 4 - step)]
                if step < 3:
                    arrive(keys[d], full.at[d, 2 - step])
                    p[zrows(sign * step, h), :] += full[d, 2 - step]
                if step == at:
                    arrive(far[d], half.at[d])
                    p[zrows(sign * step, h, d), :] += half[d]
                keys[d] = go(p.at[zrows(sign * step, h)], full.at[d, 3 - step], sign)
        yield keys, [("pf", it, s, 4)]
        for d in range(2):
            arrive(keys[d], full.at[d, 2])
        f[zrows(0, h), :] = p[zrows(0, h), :] + full[0, 2] + full[1, 2]
        mark("own_z", it, s, h)
        here = f.at[zrows(0, h)]
        keys = [go(here, here, sign) for sign in signs]
        for step in (1, 2, 3):
            for d, sign in enumerate(signs):
                yield [keys[d]], []
                block = f.at[zrows(-sign * step, h)]
                arrive(keys[d], block)
                if step == 2 and AG_SHORT:
                    part = f.at[zrows(-sign * step, h, d)]
                    far[d] = go(part, part, sign, 2)
                if step < 3:
                    keys[d] = go(block, block, sign)
                elif not AG_SHORT:
                    part = f.at[zrows(-sign * step, h, d)]
                    far[d] = go(part, part, sign)
        yield far, []
        for d in range(2):
            arrive(far[d], f.at[zrows(4, h, d)])
        mark("ff", it, s, h)

    def yrows(k, core=None, part=None):
        owner = 4 * (q if core is None else core) + (y + k + 4) % 4
        if part is None:
            return pl.ds(pl.multiple_of(16 * owner, 16), 16)
        return pl.ds(pl.multiple_of(16 * owner + 8 * part, 8), 8)

    y_links = {1: (("y", 1),), 2: (("y", 1), ("y", -1)), 3: (("y", -1),)}
    twin = {"row": 2 * y + (1 - q)}
    mine, other = pl.ds(pl.multiple_of(64 * q, 64), 64), pl.ds(pl.multiple_of(64 * (1 - q), 64), 64)
    width = NP // Y_SUBS

    def y_phase(it, s, h):
        across = pl.ds(width * h, width)
        p, f = pb.at[it, s], fb.at[it, s]
        core_half, half, full = ryc.at[it, s, h], ryh.at[it, s, h], ryf.at[it, s, h]
        signs = (1, -1)

        def go(src, dst, k):
            return message(src, dst, {"row": 2 * ((y + k) % 4) + q}, y_links[k], 1, LAT + (0.6 if k == 2 else 0.0))

        def pass_on(k):
            block = f.at[yrows(k), across]
            return message(block, block, twin, (), 1, 0.9), k

        yield [], [("pb", it, s, part) for part in range(3) if 512 * part < width * (h + 1)]
        a = message(p.at[other, across], core_half, twin, (), 1, 0.9)
        yield [a], []
        arrive(a, core_half)
        p[mine, across] += core_half[...]
        if Y_DIRECT:
            keys = {k: go(p.at[yrows(k), across], full.at[k - 1], k) for k in (2, 1, 3)}
            yield list(keys.values()), []
            total = p[yrows(0), across]
            for k in (1, 3, 2):
                arrive(keys[k], full.at[k - 1])
                total = total + full[k - 1]
        else:
            far = [go(p.at[yrows(2, None, d), across], half.at[d], sign % 4) for d, sign in enumerate(signs)]
            keys = [None, None]
            for d, sign in enumerate(signs):
                yield [far[d]], []
                arrive(far[d], half.at[d])
                p[yrows(sign, None, d), across] += half[d]
                keys[d] = go(p.at[yrows(sign), across], full.at[d], sign % 4)
            yield keys, []
            total = p[yrows(0), across]
            for d in range(2):
                arrive(keys[d], full.at[d])
                total = total + full[d]
        f[yrows(0), across] = total
        mark("own_y", it, s, h)
        here = f.at[yrows(0), across]
        if Y_DIRECT:
            keys = {k: go(here, here, k) for k in (2, 1, 3)}
            twins = [pass_on(0)]
            for k in (1, 3, 2):
                yield [keys[k]], []
                arrive(keys[k], f.at[yrows(-k), across])
                twins.append(pass_on(-k))
        else:
            keys = [go(here, here, sign % 4) for sign in signs]
            twins = [pass_on(0)]
            for d, sign in enumerate(signs):
                yield [keys[d]], []
                arrive(keys[d], f.at[yrows(-sign), across])
                part = f.at[yrows(-sign, None, d), across]
                far[d] = go(part, part, sign % 4)
                twins.append(pass_on(-sign))
            yield far, []
            for d in range(2):
                arrive(far[d], f.at[yrows(2, None, d), across])
            twins.append(pass_on(2))
        yield [k for k, _ in twins], []
        for k, place in twins:
            arrive(k, f.at[yrows(place, core=1 - q), across])
        mark("fb", it, s, h)

    norms = {}

    def exchange(n, names, needs, tiles):
        yield [], needs
        value = tiles()
        rows = 8 * len(names)
        for stage, (slots, size, me, group, hops) in enumerate(
            ((rrow, 8, row, row_peers, 2), (rcol, 8, col, col_peers, 4), (rfreq, 4, freq, freq_peers, 2))
        ):
            sbuf[n, stage, pl.ds(0, rows), :] = value
            slots[n, me, pl.ds(0, rows), :] = value
            order = sorted(range(size - 1), key=lambda k: abs(2 * k + 2 - size))
            keys = {
                k: message(sbuf.at[n, stage, pl.ds(0, rows)], slots.at[n, me, pl.ds(0, rows)], group[k], (), hops, X_LAT)
                for k in order
            }
            yield list(keys.values()), []
            for k, key in keys.items():
                arrive(key, slots.at[n, (me + size - k - 1) % size, pl.ds(0, rows)])
            value = slots[n, 0, pl.ds(0, rows), :]
            for j in range(1, size):
                value = value + slots[n, j, pl.ds(0, rows), :]
        for i, name in enumerate(names):
            norms[name] = full_sum(value[8 * i : 8 * i + 8])
        mark("x", n)

    def lanes(b):
        return pl.ds(128 * b, 128)

    def set_weights(s, value):
        xs[pl.ds(0, NP, 2), :] = value
        xs[pl.ds(1, NP, 2), :] = -turn(value)
        for b in range(24):
            wt[s, :, 128 * b : 128 * b + 128] = xs[128 * b : 128 * b + 128, :].T.astype(BF16)
        plan.now += 0.4

    loaded = []

    def fetched(part):
        for j in range(4 * part, 4 * part + 4):
            loads[j].wait()
            if j < 11:
                en[j, pl.ds(2 * N, 72), :] = jnp.zeros((72, 128), BF16)
            else:
                en[11] = jnp.pad(tail[...], ((0, 72), (0, 128 - LAST)))
        loaded.append(part)

    def adjoint(it, s):
        for part in range(3):
            yield [], []
            if part not in loaded:
                fetched(part)
            block = jnp.concatenate([en[4 * part + j] for j in range(4)], axis=1)
            pb[it, s, :, 512 * part : 512 * part + 512] = dot(wt[s], block)
            plan.now += 0.5
            mark("pb", it, s, part)

    def set_operand(s, value):
        for b in range(12):
            z[s, 128 * b : 128 * b + 128, :] = value(b).T.astype(BF16)
        plan.now += 0.2

    def forward_chunk(it, s, k, i):
        c = (col + k) % 8
        rows = pl.ds(pl.multiple_of(2 * ZC * c, 128), 2 * ZC)
        xc[i] = dot(jnp.concatenate([en[j, rows, :] for j in range(12)], axis=1), z[s])
        even, odd = xc[i, pl.ds(0, ZC, 2), :], xc[i, pl.ds(1, ZC, 2), :]
        pf[it, s, pl.ds(pl.multiple_of(ZC * c, 64), ZC), :] = even + turn(odd)

    def forward(it, s):
        for group, (first, step, count) in enumerate(((4, 0, 1), (3, 2, 2), (2, 4, 2), (1, 6, 2), (0, 0, 1))):
            yield [], []
            for i in range(count):
                forward_chunk(it, s, first + step * i, i)
            plan.now += 0.4 * count
            mark("pf", it, s, group)

    recorded.wait()
    xs[pl.ds(0, 2 * N), :] = rec[...].astype(F32)
    xs[pl.ds(2 * N, 72), :] = jnp.zeros((72, 128), F32)
    lane = lax.broadcasted_iota(jnp.int32, (NP, 128), 1)
    re, im = xs[pl.ds(0, NP, 2), :], xs[pl.ds(1, NP, 2), :]
    u[0] = jnp.where(lane < 64, re, pltpu.roll(im, 64, 1))
    u[1] = jnp.where(lane < 64, pltpu.roll(re, 64, 1), im)
    set_weights(0, u[0])
    set_weights(1, u[1])

    def own_rows(ref):
        return ref[pl.ds(pl.multiple_of(ZC * col, 64), ZC), :]

    def square_sum(values):
        return tile_sum(values[0] * values[0]) + tile_sum(values[1] * values[1])

    val = {}

    def tiles0():
        own = [fb[0, s, yrows(0), :] for s in range(2)]
        return jnp.concatenate([square_sum([own_rows(u.at[s]) for s in range(2)]), square_sum(own)], axis=0)

    def after0():
        if "k1" not in val:
            val["beta1"] = jnp.sqrt(norms["beta1"] + EPS)
            val["alpha1"] = jnp.sqrt(norms["alpha1"] / (val["beta1"] * val["beta1"]) + EPS)
            val["k1"] = 1.0 / (val["beta1"] * val["alpha1"])
            val["k2"] = val["alpha1"] / val["beta1"]

    def own_update(s):
        after0()
        return own_rows(ff.at[0, s]) * val["k1"] - own_rows(u.at[s]) * val["k2"]

    def tiles1():
        return square_sum([own_update(s) for s in range(2)])

    def after1():
        if "ib2" not in val:
            val["beta2"] = jnp.sqrt(norms["beta2"] + EPS)
            val["ib2"] = 1.0 / val["beta2"]
            val["k3"] = val["beta2"] * val["k1"]

    def tiles2():
        after1()
        return square_sum([fb[1, s, yrows(0), :] * val["ib2"] - fb[0, s, yrows(0), :] * val["k3"] for s in range(2)])

    def after2():
        if "ia2" not in val:
            val["alpha2"] = jnp.sqrt(norms["alpha2"] + EPS)
            val["ia2"] = 1.0 / val["alpha2"]

    def tiles3():
        after2()
        ratio = val["alpha2"] * val["ib2"]
        return square_sum([own_rows(ff.at[1, s]) * val["ia2"] - own_update(s) * ratio for s in range(2)])

    def work(s):
        yield from adjoint(0, s)
        yield [], [("fb", 0, s, h) for h in range(Y_SUBS)]
        set_operand(s, lambda b: fb[0, s, :, lanes(b)])
        yield from forward(0, s)
        yield [], [("x", 0)] + [("ff", 0, s, h) for h in range(SUBS)]
        after0()
        set_weights(s, ff[0, s] * val["k1"] - u[s] * val["k2"])
        yield from adjoint(1, s)
        yield [], [("x", 1)] + [("fb", 1, s, h) for h in range(Y_SUBS)]
        after1()
        set_operand(s, lambda b: fb[1, s, :, lanes(b)] * val["ib2"] - fb[0, s, :, lanes(b)] * val["k3"])
        yield from forward(1, s)

    def finish():
        yield [], [("x", 3)]
        beta1, alpha1, beta2, alpha2 = val["beta1"], val["alpha1"], val["beta2"], val["alpha2"]
        beta3 = jnp.sqrt(norms["beta3"] + EPS)
        rho1 = jnp.sqrt(alpha1 * alpha1 + beta2 * beta2)
        cos1, sin1 = alpha1 / rho1, beta2 / rho1
        gain1 = cos1 * beta1 / rho1
        ratio = sin1 * alpha2 / rho1
        rho_bar = -cos1 * alpha2
        rho2 = jnp.sqrt(rho_bar * rho_bar + beta3 * beta3)
        gain2 = rho_bar / rho2 * (sin1 * beta1) / rho2
        first, second = (gain1 - gain2 * ratio) * val["k1"], gain2 * val["ia2"]
        second_a, second_b = second * val["ib2"], first - second * val["k3"]
        for part in range(2):
            for b in range(12):
                rows = pl.ds(64 * part, 64)
                block = jnp.concatenate(
                    [fb[1, s, rows, lanes(b)] * second_a + fb[0, s, rows, lanes(b)] * second_b for s in range(2)], axis=0)
                length = 128 if b < 11 else LAST
                sol[pl.ds(256 * b + part, length, 2), :] = block.T[:length]
        plan.now += 1.0
        yield [], [("ff", 1, s, h) for s in range(2) for h in range(SUBS)]
        lane = lax.broadcasted_iota(jnp.int32, (N, 128), 1)
        out = [
            u[s, pl.ds(0, N), :] - ff[0, s, pl.ds(0, N), :] * first - ff[1, s, pl.ds(0, N), :] * second
            for s in range(2)
        ]
        res[pl.ds(0, N, 2), :] = jnp.where(lane < 64, out[0], pltpu.roll(out[1], 64, 1))
        res[pl.ds(1, N, 2), :] = jnp.where(lane < 64, pltpu.roll(out[0], 64, 1), out[1])
        plan.now += 0.5

    both = [(s, h) for s in range(2) for h in range(SUBS)]
    both_y = [(s, h) for s in range(2) for h in range(Y_SUBS)]
    streams = [z_phase(it, s, h) for it in range(2) for s, h in both]
    streams += [y_phase(it, s, h) for it in range(2) for s, h in both_y]
    streams.append(exchange(0, ("beta1", "alpha1"), [("own_y", 0, s, h) for s, h in both_y], tiles0))
    streams.append(exchange(1, ("beta2",), [("x", 0)] + [("own_z", 0, s, h) for s, h in both], tiles1))
    streams.append(exchange(2, ("alpha2",), [("x", 1)] + [("own_y", 1, s, h) for s, h in both_y], tiles2))
    streams.append(exchange(3, ("beta3",), [("x", 2)] + [("own_z", 1, s, h) for s, h in both], tiles3))
    streams += [work(0), work(1), finish()]
    plan.run(streams)
    assert len(sent) <= MESSAGES
    for copy in sent[-BEHIND:]:
        copy.wait_send()


def shards(operator, recorded):
    op = jnp.transpose(operator[0], (1, 0, 2))
    rec = jnp.transpose(recorded[0], (1, 0, 2)).reshape(2 * N, 128)
    vmem = pl.BlockSpec(memory_space=pltpu.VMEM)
    out = jax.ShapeDtypeStruct((2 * N, 128), F32)
    sol, res = pl.pallas_call(
        kernel,
        out_shape=[out, out],
        in_specs=[pl.BlockSpec(memory_space=pl.ANY)] * 2,
        out_specs=[vmem, vmem],
        scratch_shapes=[
            pltpu.VMEM((2 * N, 128), BF16),
            pltpu.VMEM((12, 2 * NP, 128), BF16),
            pltpu.VMEM((2 * N, LAST), BF16),
            pltpu.VMEM((2 * NP, 128), F32),
            pltpu.VMEM((2, 2 * ZC, 128), F32),
            pltpu.VMEM((2, NP, 128), F32),
            pltpu.VMEM((2, 128, 2 * NP), BF16),
            pltpu.VMEM((2, NP, 128), BF16),
            pltpu.VMEM((2, 2, 128, NP), F32),
            pltpu.VMEM((2, 2, 128, NP), F32),
            pltpu.VMEM((2, 2, NP, 128), F32),
            pltpu.VMEM((2, 2, NP, 128), F32),
            pltpu.VMEM((2, 2, SUBS, 2, ZC // SUBS // 2, 128), F32),
            pltpu.VMEM((2, 2, SUBS, 2, 3, ZC // SUBS, 128), F32),
            pltpu.VMEM((2, 2, Y_SUBS, 64, NP // Y_SUBS), F32),
            pltpu.VMEM((2, 2, Y_SUBS, 2, 8, NP // Y_SUBS), F32),
            pltpu.VMEM((2, 2, Y_SUBS, 3, 16, NP // Y_SUBS), F32),
            pltpu.VMEM((4, 3, 16, 128), F32),
            pltpu.VMEM((4, 8, 16, 128), F32),
            pltpu.VMEM((4, 8, 16, 128), F32),
            pltpu.VMEM((4, 4, 16, 128), F32),
            pltpu.SemaphoreType.DMA((13,)),
            pltpu.SemaphoreType.DMA((MESSAGES,)),
            pltpu.SemaphoreType.DMA((MESSAGES,)),
        ],
        compiler_params=pltpu.CompilerParams(
            collective_id=0, has_side_effects=True, vmem_limit_bytes=48 * 2**20),
        cost_estimate=pl.CostEstimate(flops=9_437_184_000, bytes_accessed=13_000_000, transcendentals=0),
    )(op, rec)
    return tuple(jnp.transpose(o.reshape(N, 2, 128), (1, 0, 2))[None] for o in (sol, res))


def solution(mesh):
    in_specs = (P("freq", None, "row", "col"), P("freq", None, "row", None))
    out_specs = (P("freq", None, "col", None), P("freq", None, "row", None))
    return jax.shard_map(shards, mesh=mesh, in_specs=in_specs, out_specs=out_specs, check_vma=False)
```
